32 devices in a mesh: clus: 32 (over z, y, x, core).
Axes of the slice: x: 2, y: 2, z: 4, core: 2. Of those that a mesh axis runs over, the one named last changes fastest.
Arguments:
- charges: float32 [32, 262144], P(None, 'clus'), may hold values from -6 to 6
- positions: float32 [3, 262144], P(None, 'clus'), may hold values from -2 to 2
- quad_weights: float32 [262144], P('clus'), may hold values from 0.1 to 1
- leaf_basis: float32 [1024, 64, 256], P('clus'), may hold values from -0.375 to 0.375
- leaf_nodes: float32 [3, 65536], P(None, 'clus'), may hold values from -2 to 2
- leaf_transfer: float32 [64, 65536], P(None, 'clus'), may hold values from -0.75 to 0.75
- mid_nodes: float32 [3, 2048], P(None, 'clus'), may hold values from -2 to 2
- mid_transfer: float32 [64, 2048], P(None, 'clus'), may hold values from -0.75 to 0.75
- top_nodes: float32 [3, 256], replicated, may hold values from -2 to 2
- near_list: int32 [1024, 27], P('clus'), may hold values from 0 to 1023, as said below
- near_count: int32 [1024], P('clus'), may hold values from 1 to 27, as said below
- far_list: int32 [1024, 16], P('clus'), may hold values from 0 to 1023, as said below
- mid_mask: int32 [32, 32], P('clus'), may hold values 0 or 1
- top_mask: int32 [4, 4], replicated, may hold values 0 or 1
Outputs:
- potential: float32 [32, 262144], P(None, 'clus')
The draws below stay inside these ranges and needn't reach their ends.
Inputs may be any that keep to these rules, and one draw needn't show every extreme that they name: `near_list`: every entry names a leaf of the device that owns the row's leaf or of the device just before or after it in a cycle over devices (the last device's next one being the first); the entries of one row are distinct and differ from those of the row's far_list. `far_list`: the same locality holds: sources lie on the owning device or its two cyclic neighbours; entries of one row are distinct. `near_count`: some leaf has all 27 slots live in every draw.
All inputs are finite; a program needn't handle non-finite values. No bound on the sum of `mid_mask` on one device may be relied on, other than what follows from the above.
Results may differ from the reference program's by a relative error of at most 0.0003.
Values sent between devices are 32-bit elements; how exact they have to be, the bound alone decides.
A program may use at most 128 MiB of HBM per device.

```python
import math
import jax
import jax.numpy as jnp
from jax import lax

LEAF = 256
RANK = 64
NRHS = 32
LEAF_DEV = 32
NEAR_MAX = 27
FAR2 = 16
GROUP = 8
LEAVES = 1024
POINTS = 262144
TOP = 4
N_CLUS = 32


def window_leaves(key):
    leaf_keys = jax.random.split(key, LEAVES)
    shuffled = jax.vmap(lambda single: jax.random.permutation(single, 3 * LEAF_DEV))(leaf_keys)
    leaf_index = jnp.arange(LEAVES, dtype=jnp.int32)
    first_leaf = leaf_index // LEAF_DEV * LEAF_DEV - LEAF_DEV
    return ((first_leaf[:, None] + shuffled.astype(jnp.int32)) % LEAVES).astype(jnp.int32)


def draw_near_list(key, part):
    chosen = window_leaves(key)
    return chosen[:, :NEAR_MAX]


def draw_far_list(key, part):
    chosen = window_leaves(key)
    return chosen[:, NEAR_MAX:NEAR_MAX + FAR2]


def draw_near_count(key, part):
    key = jax.random.fold_in(key, 11)
    level_key, count_key, pick_key = jax.random.split(key, 3)
    devices = LEAVES // LEAF_DEV
    levels = jax.random.randint(level_key, (devices,), NEAR_MAX // 4 + 1, NEAR_MAX + 1)
    per_leaf = jnp.repeat(levels, LEAF_DEV)
    counts = jax.random.randint(count_key, (LEAVES,), per_leaf // 2 + 1, per_leaf + 1)
    picked = jax.random.randint(pick_key, (), 0, LEAVES)
    counts = jnp.where(jnp.arange(LEAVES) == picked, NEAR_MAX, counts)
    return counts.astype(jnp.int32)


def set_ends(array, own_key, low, high):
    longest = array.shape.index(max(array.shape))
    spots = []
    for shift in (0, 1):
        where = [jax.random.randint(jax.random.fold_in(own_key, axis), (), 0, length) for axis, length in enumerate(array.shape)]
        where[longest] = (where[longest] + shift) % array.shape[longest]
        spots.append(tuple(where))
    return array.at[spots[0]].set(low).at[spots[1]].set(high)


def block_scale(own_key, shape, pieces, smallest, largest):
    level, own = 1.0, jax.random.fold_in(own_key, 6)
    for position, blocks in pieces:
        steps = jnp.exp(jax.random.uniform(jax.random.fold_in(own, position), (blocks,), jnp.float32, smallest / len(pieces), largest / len(pieces)))
        level = level * jnp.repeat(steps, shape[position] // blocks).reshape([-1 if axis == position else 1 for axis in range(len(shape))])
    return level


def centred(stream_key, extent, scale, bound, cuts=(), kind=jnp.bfloat16):
    drawn = jax.random.normal(stream_key, extent, jnp.float32) * scale
    if len(cuts) > 0:
        drawn = block_scale(stream_key, extent, cuts, -0.22, 0.18) * drawn
    return jnp.clip(drawn, min=-bound, max=bound).astype(kind)


def setup_inputs(seed: int = 0) -> dict:
    keys = jax.random.split(jax.random.key(seed), 15)
    charges = centred(keys[0], (NRHS, POINTS), 1.0, 6.0, ((1, 32),), jnp.float32)
    positions = jnp.clip(jax.random.uniform(keys[1], (3, POINTS), jnp.float32, -2.0, 2.0) * block_scale(keys[1], (3, POINTS), ((1, 32),), -0.4, 0.0), -2.0, 2.0)
    quad_weights = jnp.clip(jnp.exp(math.log(1.0) - 2.3025851 * jax.random.uniform(keys[2], (POINTS,), jnp.float32) ** block_scale(keys[2], (POINTS,), ((0, 32),), -0.2, 0.2)), 0.1, 1.0)
    leaf_basis = centred(keys[3], (LEAVES, RANK, LEAF), LEAF ** -0.5, 0.375, ((0, 32),), jnp.float32)
    leaf_nodes = jnp.clip(jax.random.uniform(keys[4], (3, LEAVES * RANK), jnp.float32, -2.0, 2.0) * block_scale(keys[4], (3, LEAVES * RANK), ((1, 32),), -0.4, 0.0), -2.0, 2.0)
    leaf_transfer = centred(keys[5], (RANK, LEAVES * RANK), RANK ** -0.5, 0.75, ((1, 32),), jnp.float32)
    mid_nodes = jnp.clip(jax.random.uniform(keys[6], (3, N_CLUS * RANK), jnp.float32, -2.0, 2.0) * block_scale(keys[6], (3, N_CLUS * RANK), ((1, 32),), -0.4, 0.0), -2.0, 2.0)
    mid_transfer = centred(keys[7], (RANK, N_CLUS * RANK), RANK ** -0.5, 0.75, ((1, 32),), jnp.float32)
    top_nodes = jnp.clip(jax.random.uniform(keys[8], (3, TOP * RANK), jnp.float32, -2.0, 2.0), -2.0, 2.0)
    near_list = draw_near_list(jax.random.fold_in(keys[14], 71), 0)
    near_count = draw_near_count(jax.random.fold_in(keys[14], 71), 0)
    far_list = draw_far_list(jax.random.fold_in(keys[14], 71), 0)
    mid_mask = set_ends((jax.random.randint(keys[12], (N_CLUS, N_CLUS), 0, 4) < 1).astype(jnp.int32), jax.random.fold_in(keys[12], 1), 0, 1)
    top_mask = set_ends((jax.random.randint(keys[13], (TOP, TOP), 0, 2) < 1).astype(jnp.int32), jax.random.fold_in(keys[13], 1), 0, 1)
    return {"charges": charges, "positions": positions, "quad_weights": quad_weights, "leaf_basis": leaf_basis, "leaf_nodes": leaf_nodes, "leaf_transfer": leaf_transfer, "mid_nodes": mid_nodes, "mid_transfer": mid_transfer, "top_nodes": top_nodes, "near_list": near_list, "near_count": near_count, "far_list": far_list, "mid_mask": mid_mask, "top_mask": top_mask}


smoothing = 0.05
inv_four_pi = 1.0 / (4.0 * math.pi)
highest = lax.Precision.HIGHEST

def green(source, target):
    first = source[0][..., :, None] - target[0][..., None, :]
    second = source[1][..., :, None] - target[1][..., None, :]
    third = source[2][..., :, None] - target[2][..., None, :]
    total = first * first + second * second + third * third
    return inv_four_pi / jnp.sqrt(total + smoothing * smoothing)

def reference(charges, positions, quad_weights, leaf_basis, leaf_nodes, leaf_transfer, mid_nodes, mid_transfer, top_nodes, near_list, near_count, far_list, mid_mask, top_mask):
    leaf_charges = charges.reshape(NRHS, LEAVES, LEAF)
    leaf_points = positions.reshape(3, LEAVES, LEAF)
    leaf_weights = quad_weights.reshape(LEAVES, LEAF)
    leaf_coef = jnp.einsum('rlb,lkb->rlk', leaf_charges, leaf_basis, precision=highest)
    block_coef = leaf_coef.reshape(NRHS, N_CLUS, LEAF_DEV * RANK)
    transfer_blocks = leaf_transfer.reshape(RANK, N_CLUS, LEAF_DEV * RANK)
    mid_coef = jnp.einsum('rpj,qpj->rpq', block_coef, transfer_blocks, precision=highest)
    mid_blocks = mid_transfer.reshape(RANK, N_CLUS, RANK)
    upward = jnp.einsum('rpk,qpk->rpq', mid_coef, mid_blocks, precision=highest)
    top_coef = upward.reshape(NRHS, TOP, GROUP, RANK).sum(axis=2).reshape(NRHS, TOP * RANK)
    top_kernel = green(top_nodes, top_nodes)
    top_select = jnp.repeat(jnp.repeat(top_mask.T.astype(jnp.float32), RANK, axis=0), RANK, axis=1)
    top_field = jnp.dot(top_coef, top_kernel * top_select, precision=highest).reshape(NRHS, TOP, RANK)
    mid_flat = mid_coef.reshape(NRHS, N_CLUS * RANK)

    def mid_one(cluster):
        target = lax.dynamic_slice_in_dim(mid_nodes, cluster * RANK, RANK, 1)
        select = jnp.repeat(mid_mask[cluster].astype(jnp.float32), RANK)[:, None]
        return jnp.dot(mid_flat, green(mid_nodes, target) * select, precision=highest)
    mid_field = jnp.transpose(lax.map(mid_one, jnp.arange(N_CLUS)), (1, 0, 2))
    top_down = jnp.repeat(top_field, GROUP, axis=1)
    mid_field = mid_field + jnp.einsum('rpq,qpk->rpk', top_down, mid_blocks, precision=highest)
    leaf_down = jnp.einsum('rpq,qpj->rpj', mid_field, transfer_blocks, precision=highest)
    leaf_down = leaf_down.reshape(NRHS, LEAVES, RANK)
    node_blocks = leaf_nodes.reshape(3, LEAVES, RANK)

    def block_work(block):
        first_leaf = block * LEAF_DEV
        far_rows = lax.dynamic_slice_in_dim(far_list, first_leaf, LEAF_DEV, 0)
        source_coef = jnp.take(leaf_coef, far_rows, axis=1)
        source_nodes = jnp.take(node_blocks, far_rows, axis=1)
        target_nodes = lax.dynamic_slice_in_dim(node_blocks, first_leaf, LEAF_DEV, 1)
        coupling = green(source_nodes, target_nodes[:, :, None, :])
        far_field = jnp.einsum('rlfj,lfji->rli', source_coef, coupling, precision=highest)
        far_field = far_field + lax.dynamic_slice_in_dim(leaf_down, first_leaf, LEAF_DEV, 1)
        own_basis = lax.dynamic_slice_in_dim(leaf_basis, first_leaf, LEAF_DEV, 0)
        far_out = jnp.einsum('rlk,lkb->rlb', far_field, own_basis, precision=highest)
        near_rows = lax.dynamic_slice_in_dim(near_list, first_leaf, LEAF_DEV, 0)
        counts = lax.dynamic_slice_in_dim(near_count, first_leaf, LEAF_DEV, 0)
        target_points = lax.dynamic_slice_in_dim(leaf_points, first_leaf, LEAF_DEV, 1)

        def slot(index, total):
            chosen = lax.dynamic_index_in_dim(near_rows, index, 1, keepdims=False)
            live = (index < counts).astype(jnp.float32)
            source_points = jnp.take(leaf_points, chosen, axis=1)
            weighted = jnp.take(leaf_weights, chosen, axis=0) * live[:, None]
            block_kernel = green(source_points, target_points) * weighted[:, :, None]
            source_charges = jnp.take(leaf_charges, chosen, axis=1)
            return total + jnp.einsum('rlb,lba->rla', source_charges, block_kernel, precision=highest)
        near_out = lax.fori_loop(0, NEAR_MAX, slot, jnp.zeros((NRHS, LEAF_DEV, LEAF), jnp.float32))
        return far_out + near_out
    result = lax.map(block_work, jnp.arange(N_CLUS))
    return jnp.transpose(result, (1, 0, 2, 3)).reshape(NRHS, POINTS)
```

```python
import math

import jax
import jax.numpy as jnp
from jax import lax
from jax.experimental import pallas as pl
from jax.experimental.pallas import tpu as pltpu
from jax.sharding import PartitionSpec as P

LEAF = 256
RANK = 64
NRHS = 32
LEAF_DEV = 32
NEAR_MAX = 27
FAR2 = 16
GROUP = 8
FEAT = 48


smoothing = 0.05
inv_four_pi = 1.0 / (4.0 * math.pi)
highest = lax.Precision.HIGHEST
f32 = jnp.float32
bf16 = jnp.bfloat16


def green(source, target):
    first = source[0][..., :, None] - target[0][..., None, :]
    second = source[1][..., :, None] - target[1][..., None, :]
    third = source[2][..., :, None] - target[2][..., None, :]
    total = first * first + second * second + third * third
    return inv_four_pi / jnp.sqrt(total + smoothing * smoothing)


def rounded(value):
    return value.astype(bf16).astype(f32)


def split3(value):
    high = rounded(value)
    rest = value - high
    mid = rounded(rest)
    return high, mid, rounded(rest - mid)


def centred_rows(x, y, z, centre):
    x = x - centre[0]
    y = y - centre[1]
    z = z - centre[2]
    return x, y, z, x * x + y * y + z * z


def rows8(values):
    width = values[0].shape[1]
    row = lax.broadcasted_iota(jnp.int32, (8, width), 0)
    out = jnp.zeros((8, width), f32)
    for place, value in enumerate(values):
        out = jnp.where(row == place, value, out)
    return out


def source_features(x, y, z, centre):
    x, y, z, norm = centred_rows(x, y, z, centre)
    high, mid, low = split3(rows8([x, y, z, norm, jnp.ones_like(x)]))
    return jnp.concatenate([high, mid, low, high, mid, high], axis=0)


def target_features(x, y, z, centre):
    x, y, z, norm = centred_rows(x, y, z, centre)
    high, mid, low = split3(
        rows8([-2.0 * x, -2.0 * y, -2.0 * z, jnp.ones_like(x), norm + smoothing * smoothing])
    )
    return jnp.concatenate([high, high, high, mid, mid, low], axis=0)


def halves(value):
    high = value.astype(bf16)
    return high, (value - high.astype(f32)).astype(bf16)


def field(coef, features, target):
    inverse = lax.rsqrt(jnp.dot(features, target, preferred_element_type=f32))
    high, low = halves(inverse)
    first = jnp.dot(coef, high, preferred_element_type=f32)
    second = jnp.dot(coef[:NRHS], low, preferred_element_type=f32)
    return first[:NRHS] + first[NRHS:] + second


def couple(
    near_ref,
    count_ref,
    far_ref,
    before_ref,
    own_ref,
    after_ref,
    coef_before_ref,
    coef_own_ref,
    coef_after_ref,
    near_out,
    far_out,
    point_source,
    point_target,
    charge_store,
    node_source,
    node_target,
    coef_left,
    coef_right,
):
    sums = [jnp.sum(own_ref[NRHS + d : NRHS + d + 1, :], axis=1, keepdims=True) for d in range(3)]
    centre = [total * (1.0 / (LEAF_DEV * LEAF)) for total in sums]
    lane = lax.broadcasted_iota(jnp.int32, (2 * NRHS, 128), 1)
    charge_store[3 * LEAF_DEV] = jnp.zeros((2 * NRHS, LEAF), bf16)
    pairs = LEAF_DEV // 2

    for part, (pack, coefs) in enumerate(
        [(before_ref, coef_before_ref), (own_ref, coef_own_ref), (after_ref, coef_after_ref)]
    ):

        def prepare(leaf, carry, pack=pack, part=part):
            columns = pl.ds(pl.multiple_of(leaf * LEAF, LEAF), LEAF)
            place = part * LEAF_DEV + leaf
            x, y, z, weight = [pack[NRHS + d : NRHS + d + 1, columns] for d in range(4)]
            point_source[place] = source_features(x, y, z, centre).T.astype(bf16)
            if part == 1:
                point_target[leaf] = target_features(x, y, z, centre).astype(bf16)
            high, low = halves(pack[:NRHS, columns] * (weight * inv_four_pi))
            charge_store[place, :NRHS, :] = high
            charge_store[place, NRHS:, :] = low
            return carry

        lax.fori_loop(0, LEAF_DEV, prepare, 0)

        def prepare_nodes(pair, carry, coefs=coefs, part=part):
            columns = pl.ds(pl.multiple_of(pair * 128, 128), 128)
            place = part * LEAF_DEV + pair * 2
            x, y, z = [coefs[NRHS + d : NRHS + d + 1, columns] for d in range(3)]
            features = source_features(x, y, z, centre).T.astype(bf16)
            node_source[place] = features[:RANK]
            node_source[place + 1] = features[RANK:]
            if part == 1:
                node_target[pair] = target_features(x, y, z, centre).astype(bf16)
            high = rounded(coefs[:NRHS, columns] * inv_four_pi)
            low = coefs[:NRHS, columns] * inv_four_pi - high
            both = jnp.concatenate([high, low], axis=0)
            turned = pltpu.roll(both, RANK, 1)
            left = lane < RANK
            coef_left[place] = jnp.where(left, both, 0.0).astype(bf16)
            coef_right[place] = jnp.where(left, 0.0, turned).astype(bf16)
            coef_left[place + 1] = jnp.where(left, turned, 0.0).astype(bf16)
            coef_right[place + 1] = jnp.where(left, 0.0, both).astype(bf16)
            return carry

        lax.fori_loop(0, pairs, prepare_nodes, 0)

    def near(leaf):
        count = count_ref[leaf]
        target = point_target[leaf]

        def slots(step, total):
            for offset in range(2):
                slot = step * 2 + offset
                source = near_ref[leaf, jnp.minimum(slot, NEAR_MAX - 1)]
                charge = jnp.where(slot < count, source, 3 * LEAF_DEV)
                total = total + field(charge_store[charge], point_source[source], target)
            return total

        return lax.fori_loop(0, (count + 1) // 2, slots, jnp.zeros((NRHS, LEAF), f32))

    def far(leaf, pair):
        sources = [far_ref[leaf, slot] for slot in range(FAR2)]
        features = jnp.concatenate([node_source[source] for source in sources], axis=0)
        coef = jnp.concatenate(
            [coef_left[sources[i]] + coef_right[sources[i + 1]] for i in range(0, FAR2, 2)], axis=1
        )
        return field(coef, features, node_target[pair])

    def work(pair, carry):
        for offset in range(2):
            leaf = pair * 2 + offset
            near_out[:, pl.ds(pl.multiple_of(leaf * LEAF, LEAF), LEAF)] = near(leaf)
        even, odd = far(pair * 2, pair), far(pair * 2 + 1, pair)
        columns = pl.ds(pl.multiple_of(pair * 128, 128), 128)
        far_out[:, columns] = jnp.where(lane[:NRHS] < RANK, even, odd)
        return carry

    lax.fori_loop(0, pairs, work, 0)


def coupled(near_local, near_count, far_local, points, coefs):
    window = 3 * LEAF_DEV
    smem = pl.BlockSpec(memory_space=pltpu.SMEM)
    vmem = pl.BlockSpec(memory_space=pltpu.VMEM)
    return pl.pallas_call(
        couple,
        out_shape=(
            jax.ShapeDtypeStruct((NRHS, LEAF_DEV * LEAF), f32),
            jax.ShapeDtypeStruct((NRHS, LEAF_DEV * RANK), f32),
        ),
        in_specs=[smem] * 3 + [vmem] * 6,
        out_specs=(vmem, vmem),
        scratch_shapes=[
            pltpu.VMEM((window, LEAF, FEAT), bf16),
            pltpu.VMEM((LEAF_DEV, FEAT, LEAF), bf16),
            pltpu.VMEM((window + 1, 2 * NRHS, LEAF), bf16),
            pltpu.VMEM((window, RANK, FEAT), bf16),
            pltpu.VMEM((LEAF_DEV // 2, FEAT, 128), bf16),
            pltpu.VMEM((window, 2 * NRHS, 128), bf16),
            pltpu.VMEM((window, 2 * NRHS, 128), bf16),
        ],
        compiler_params=pltpu.CompilerParams(vmem_limit_bytes=48 * 1024 * 1024),
        cost_estimate=pl.CostEstimate(
            flops=40_000_000_000, bytes_accessed=8_000_000, transcendentals=50_000_000
        ),
    )(near_local, near_count, far_local, *points, *coefs)


def around(array):
    size = lax.axis_size("clus")
    up = [(i, (i + 1) % size) for i in range(size)]
    down = [(j, i) for i, j in up]
    return lax.ppermute(array, "clus", up), array, lax.ppermute(array, "clus", down)


def shards(
    charges,
    positions,
    quad_weights,
    leaf_basis,
    leaf_nodes,
    leaf_transfer,
    mid_nodes,
    mid_transfer,
    top_nodes,
    near_list,
    near_count,
    far_list,
    mid_mask,
    top_mask,
):
    devices = lax.axis_size("clus")
    myself = lax.axis_index("clus")
    all_leaves = LEAF_DEV * devices
    top_count = devices // GROUP
    point_pack = jnp.concatenate([charges, positions, quad_weights[None, :]], axis=0)
    points = around(point_pack)
    leaf_charges = charges.reshape(NRHS, LEAF_DEV, LEAF)
    leaf_coef = jnp.einsum("rlb,lkb->rlk", leaf_charges, leaf_basis, precision=highest)
    coef_flat = leaf_coef.reshape(NRHS, LEAF_DEV * RANK)
    coefs = around(jnp.concatenate([coef_flat, leaf_nodes], axis=0))
    contract_last = (((1,), (1,)), ((), ()))
    mid_coef = lax.dot_general(coef_flat, leaf_transfer, contract_last, precision=highest)
    upward = lax.dot_general(mid_coef, mid_transfer, contract_last, precision=highest)
    level_pack = jnp.concatenate([mid_coef, upward, mid_nodes], axis=0)
    everyone = lax.all_gather(level_pack, "clus", axis=1, tiled=True)

    first_leaf = myself * LEAF_DEV - LEAF_DEV
    near_local = (near_list - first_leaf) % all_leaves
    far_local = (far_list - first_leaf) % all_leaves
    near_out, far_field = coupled(near_local, near_count, far_local, points, coefs)

    all_coef = everyone[:NRHS]
    all_upward = everyone[NRHS : 2 * NRHS].reshape(NRHS, top_count, GROUP, RANK)
    all_nodes = everyone[2 * NRHS :]
    top_coef = all_upward.sum(axis=2).reshape(NRHS, top_count * RANK)
    parent = myself // GROUP
    top_target = lax.dynamic_slice_in_dim(top_nodes, parent * RANK, RANK, 1)
    top_row = lax.dynamic_index_in_dim(top_mask, parent, 0, keepdims=False)
    top_select = jnp.repeat(top_row.astype(jnp.float32), RANK)[:, None]
    top_field = jnp.dot(top_coef, green(top_nodes, top_target) * top_select, precision=highest)
    mid_select = jnp.repeat(mid_mask[0].astype(jnp.float32), RANK)[:, None]
    mid_field = jnp.dot(all_coef, green(all_nodes, mid_nodes) * mid_select, precision=highest)
    mid_field = mid_field + jnp.dot(top_field, mid_transfer, precision=highest)
    leaf_down = jnp.dot(mid_field, leaf_transfer, precision=highest)
    leaf_field = (far_field + leaf_down).reshape(NRHS, LEAF_DEV, RANK)
    far_out = jnp.einsum("rlk,lkb->rlb", leaf_field, leaf_basis, precision=highest)
    return far_out.reshape(NRHS, LEAF_DEV * LEAF) + near_out


def solution(mesh):
    in_specs = (
        P(None, "clus"),
        P(None, "clus"),
        P("clus"),
        P("clus", None, None),
        P(None, "clus"),
        P(None, "clus"),
        P(None, "clus"),
        P(None, "clus"),
        P(),
        P("clus", None),
        P("clus"),
        P("clus", None),
        P("clus", None),
        P(),
    )
    out_specs = P(None, "clus")
    return jax.shard_map(shards, mesh=mesh, in_specs=in_specs, out_specs=out_specs, check_vma=False)
```

```python
import math

import jax
import jax.numpy as jnp
from jax import lax
from jax.experimental import pallas as pl
from jax.experimental.pallas import tpu as pltpu
from jax.sharding import PartitionSpec as P

LEAF = 256
RANK = 64
NRHS = 32
LEAF_DEV = 32
NEAR_MAX = 27
FAR2 = 16
GROUP = 8
FEAT = 48


smoothing = 0.05
inv_four_pi = 1.0 / (4.0 * math.pi)
highest = lax.Precision.HIGHEST
f32 = jnp.float32
bf16 = jnp.bfloat16


def green(source, target):
    first = source[0][..., :, None] - target[0][..., None, :]
    second = source[1][..., :, None] - target[1][..., None, :]
    third = source[2][..., :, None] - target[2][..., None, :]
    total = first * first + second * second + third * third
    return inv_four_pi / jnp.sqrt(total + smoothing * smoothing)


def rounded(value):
    return value.astype(bf16).astype(f32)


def split3(value):
    high = rounded(value)
    rest = value - high
    mid = rounded(rest)
    return high, mid, rounded(rest - mid)


def centred_rows(x, y, z, centre):
    x = x - centre[0]
    y = y - centre[1]
    z = z - centre[2]
    return x, y, z, x * x + y * y + z * z


def rows8(values):
    width = values[0].shape[1]
    row = lax.broadcasted_iota(jnp.int32, (8, width), 0)
    out = jnp.zeros((8, width), f32)
    for place, value in enumerate(values):
        out = jnp.where(row == place, value, out)
    return out


def source_features(x, y, z, centre):
    x, y, z, norm = centred_rows(x, y, z, centre)
    high, mid, low = split3(rows8([x, y, z, norm, jnp.ones_like(x)]))
    return jnp.concatenate([high, mid, low, high, mid, high], axis=0)


def target_features(x, y, z, centre):
    x, y, z, norm = centred_rows(x, y, z, centre)
    high, mid, low = split3(
        rows8([-2.0 * x, -2.0 * y, -2.0 * z, jnp.ones_like(x), norm + smoothing * smoothing])
    )
    return jnp.concatenate([high, high, high, mid, mid, low], axis=0)


def halves(value):
    high = value.astype(bf16)
    return high, (value - high.astype(f32)).astype(bf16)


def kernel_halves(features, target):
    return halves(lax.rsqrt(jnp.dot(features, target, preferred_element_type=f32)))


def apply(coef, high, low):
    first = jnp.dot(coef, high, preferred_element_type=f32)
    second = jnp.dot(coef[:NRHS], low, preferred_element_type=f32)
    return first[:NRHS] + first[NRHS:] + second


def couple(
    near_ref,
    count_ref,
    far_ref,
    before_ref,
    own_ref,
    after_ref,
    coef_before_ref,
    coef_own_ref,
    coef_after_ref,
    near_out,
    far_out,
    point_source,
    point_target,
    charge_store,
    node_source,
    node_target,
    coef_left,
    coef_right,
    high_even,
    low_even,
    high_odd,
    low_odd,
):
    sums = [jnp.sum(own_ref[NRHS + d : NRHS + d + 1, :], axis=1, keepdims=True) for d in range(3)]
    centre = [total * (1.0 / (LEAF_DEV * LEAF)) for total in sums]
    lane = lax.broadcasted_iota(jnp.int32, (2 * NRHS, 128), 1)
    charge_store[3 * LEAF_DEV] = jnp.zeros((2 * NRHS, LEAF), bf16)
    high_odd[...] = jnp.zeros_like(high_odd)
    low_odd[...] = jnp.zeros_like(low_odd)
    pairs = LEAF_DEV // 2

    for part, (pack, coefs) in enumerate(
        [(before_ref, coef_before_ref), (own_ref, coef_own_ref), (after_ref, coef_after_ref)]
    ):

        def prepare(group, carry, pack=pack, part=part):
            for offset in range(4):
                leaf = group * 4 + offset
                columns = pl.ds(pl.multiple_of(leaf * LEAF, LEAF), LEAF)
                place = part * LEAF_DEV + leaf
                x, y, z, weight = [pack[NRHS + d : NRHS + d + 1, columns] for d in range(4)]
                point_source[place] = source_features(x, y, z, centre).T.astype(bf16)
                if part == 1:
                    point_target[leaf] = target_features(x, y, z, centre).astype(bf16)
                high, low = halves(pack[:NRHS, columns] * (weight * inv_four_pi))
                charge_store[place, :NRHS, :] = high
                charge_store[place, NRHS:, :] = low
            return carry

        lax.fori_loop(0, LEAF_DEV // 4, prepare, 0)

        def prepare_nodes(pair, carry, coefs=coefs, part=part):
            columns = pl.ds(pl.multiple_of(pair * 128, 128), 128)
            place = part * LEAF_DEV + pair * 2
            x, y, z = [coefs[NRHS + d : NRHS + d + 1, columns] for d in range(3)]
            features = source_features(x, y, z, centre).T.astype(bf16)
            node_source[place] = features[:RANK]
            node_source[place + 1] = features[RANK:]
            if part == 1:
                node_target[pair] = target_features(x, y, z, centre).astype(bf16)
            high = rounded(coefs[:NRHS, columns] * inv_four_pi)
            low = coefs[:NRHS, columns] * inv_four_pi - high
            both = jnp.concatenate([high, low], axis=0)
            turned = pltpu.roll(both, RANK, 1)
            left = lane < RANK
            coef_left[place] = jnp.where(left, both, 0.0).astype(bf16)
            coef_right[place] = jnp.where(left, 0.0, turned).astype(bf16)
            coef_left[place + 1] = jnp.where(left, turned, 0.0).astype(bf16)
            coef_right[place + 1] = jnp.where(left, 0.0, both).astype(bf16)
            return carry

        lax.fori_loop(0, pairs, prepare_nodes, 0)

    def near(leaf):
        count = count_ref[leaf]
        target = point_target[leaf]

        def stage(slot, high_ref, low_ref):
            source = near_ref[leaf, jnp.minimum(slot, NEAR_MAX - 1)]
            high_ref[...], low_ref[...] = kernel_halves(point_source[source], target)
            return jnp.where(slot < count, source, 3 * LEAF_DEV)

        def slots(step, carry):
            total, waiting = carry
            total = total + apply(charge_store[waiting], high_odd[...], low_odd[...])
            even = stage(step * 2, high_even, low_even)
            total = total + apply(charge_store[even], high_even[...], low_even[...])
            return total, stage(step * 2 + 1, high_odd, low_odd)

        start = (jnp.zeros((NRHS, LEAF), f32), jnp.int32(3 * LEAF_DEV))
        total, waiting = lax.fori_loop(0, (count + 1) // 2, slots, start)
        return total + apply(charge_store[waiting], high_odd[...], low_odd[...])

    def far(leaf, pair):
        sources = [far_ref[leaf, slot] for slot in range(FAR2)]
        features = jnp.concatenate([node_source[source] for source in sources], axis=0)
        coef = jnp.concatenate(
            [coef_left[sources[i]] + coef_right[sources[i + 1]] for i in range(0, FAR2, 2)], axis=1
        )
        return apply(coef, *kernel_halves(features, node_target[pair]))

    def work(pair, carry):
        for offset in range(2):
            leaf = pair * 2 + offset
            near_out[:, pl.ds(pl.multiple_of(leaf * LEAF, LEAF), LEAF)] = near(leaf)
        even, odd = far(pair * 2, pair), far(pair * 2 + 1, pair)
        columns = pl.ds(pl.multiple_of(pair * 128, 128), 128)
        far_out[:, columns] = jnp.where(lane[:NRHS] < RANK, even, odd)
        return carry

    lax.fori_loop(0, pairs, work, 0)


def coupled(near_local, near_count, far_local, points, coefs):
    window = 3 * LEAF_DEV
    smem = pl.BlockSpec(memory_space=pltpu.SMEM)
    vmem = pl.BlockSpec(memory_space=pltpu.VMEM)
    return pl.pallas_call(
        couple,
        out_shape=(
            jax.ShapeDtypeStruct((NRHS, LEAF_DEV * LEAF), f32),
            jax.ShapeDtypeStruct((NRHS, LEAF_DEV * RANK), f32),
        ),
        in_specs=[smem] * 3 + [vmem] * 6,
        out_specs=(vmem, vmem),
        scratch_shapes=[
            pltpu.VMEM((window, LEAF, FEAT), bf16),
            pltpu.VMEM((LEAF_DEV, FEAT, LEAF), bf16),
            pltpu.VMEM((window + 1, 2 * NRHS, LEAF), bf16),
            pltpu.VMEM((window, RANK, FEAT), bf16),
            pltpu.VMEM((LEAF_DEV // 2, FEAT, 128), bf16),
            pltpu.VMEM((window, 2 * NRHS, 128), bf16),
            pltpu.VMEM((window, 2 * NRHS, 128), bf16),
        ]
        + [pltpu.VMEM((LEAF, LEAF), bf16)] * 4,
        compiler_params=pltpu.CompilerParams(vmem_limit_bytes=48 * 1024 * 1024),
        cost_estimate=pl.CostEstimate(
            flops=40_000_000_000, bytes_accessed=8_000_000, transcendentals=50_000_000
        ),
    )(near_local, near_count, far_local, *points, *coefs)


def doubling(steps, block_ref, all_ref, send_sems, recv_sems):
    me = lax.axis_index("clus")
    partners = [me + (1 - 2 * ((me // 2**k) % 2)) * 2**k for k in range(steps)]
    barrier = pltpu.get_barrier_semaphore()
    for partner in partners:
        pl.semaphore_signal(
            barrier, inc=1, device_id=(partner,), device_id_type=pl.DeviceIdType.MESH
        )
    pl.semaphore_wait(barrier, steps)
    all_ref[me] = block_ref[...]
    for k, partner in enumerate(partners):
        held = all_ref.at[pl.ds((me // 2**k) * 2**k, 2**k)]
        copy = pltpu.make_async_remote_copy(
            src_ref=held,
            dst_ref=held,
            send_sem=send_sems.at[k],
            recv_sem=recv_sems.at[k],
            device_id=(partner,),
            device_id_type=pl.DeviceIdType.MESH,
        )
        copy.start()
        copy.wait()


def gathered(block):
    devices = lax.axis_size("clus")
    steps = devices.bit_length() - 1
    vmem = pl.BlockSpec(memory_space=pltpu.VMEM)
    return pl.pallas_call(
        lambda *refs: doubling(steps, *refs),
        out_shape=jax.ShapeDtypeStruct((devices,) + block.shape, f32),
        in_specs=[vmem],
        out_specs=vmem,
        scratch_shapes=[pltpu.SemaphoreType.DMA((steps,)), pltpu.SemaphoreType.DMA((steps,))],
        compiler_params=pltpu.CompilerParams(
            collective_id=0, has_side_effects=True, vmem_limit_bytes=16 * 1024 * 1024
        ),
        cost_estimate=pl.CostEstimate(flops=0, bytes_accessed=20_000_000, transcendentals=0),
    )(block)


def around(array):
    size = lax.axis_size("clus")
    up = [(i, (i + 1) % size) for i in range(size)]
    down = [(j, i) for i, j in up]
    return lax.ppermute(array, "clus", up), array, lax.ppermute(array, "clus", down)


def shards(
    charges,
    positions,
    quad_weights,
    leaf_basis,
    leaf_nodes,
    leaf_transfer,
    mid_nodes,
    mid_transfer,
    top_nodes,
    near_list,
    near_count,
    far_list,
    mid_mask,
    top_mask,
):
    devices = lax.axis_size("clus")
    myself = lax.axis_index("clus")
    all_leaves = LEAF_DEV * devices
    top_count = devices // GROUP
    point_pack = jnp.concatenate([charges, positions, quad_weights[None, :]], axis=0)
    points = around(point_pack)
    leaf_charges = charges.reshape(NRHS, LEAF_DEV, LEAF)
    leaf_coef = jnp.einsum("rlb,lkb->rlk", leaf_charges, leaf_basis, precision=highest)
    coef_flat = leaf_coef.reshape(NRHS, LEAF_DEV * RANK)
    coefs = around(jnp.concatenate([coef_flat, leaf_nodes], axis=0))
    contract_last = (((1,), (1,)), ((), ()))
    mid_coef = lax.dot_general(coef_flat, leaf_transfer, contract_last, precision=highest)
    upward = lax.dot_general(mid_coef, mid_transfer, contract_last, precision=highest)
    level_pack = jnp.concatenate([mid_coef, upward], axis=1)
    level_pack = jnp.concatenate([level_pack, jnp.pad(mid_nodes, ((0, 5), (0, RANK)))], axis=0)
    everyone = gathered(level_pack)

    first_leaf = myself * LEAF_DEV - LEAF_DEV
    near_local = (near_list - first_leaf) % all_leaves
    far_local = (far_list - first_leaf) % all_leaves
    near_out, far_field = coupled(near_local, near_count, far_local, points, coefs)

    all_coef = everyone[:, :NRHS, :RANK].transpose(1, 0, 2).reshape(NRHS, devices * RANK)
    all_upward = everyone[:, :NRHS, RANK:].reshape(top_count, GROUP, NRHS, RANK)
    all_nodes = everyone[:, NRHS : NRHS + 3, :RANK].transpose(1, 0, 2).reshape(3, devices * RANK)
    top_coef = all_upward.sum(axis=1).transpose(1, 0, 2).reshape(NRHS, top_count * RANK)
    parent = myself // GROUP
    top_target = lax.dynamic_slice_in_dim(top_nodes, parent * RANK, RANK, 1)
    top_row = lax.dynamic_index_in_dim(top_mask, parent, 0, keepdims=False)
    top_select = jnp.repeat(top_row.astype(jnp.float32), RANK)[:, None]
    top_field = jnp.dot(top_coef, green(top_nodes, top_target) * top_select, precision=highest)
    mid_select = jnp.repeat(mid_mask[0].astype(jnp.float32), RANK)[:, None]
    mid_field = jnp.dot(all_coef, green(all_nodes, mid_nodes) * mid_select, precision=highest)
    mid_field = mid_field + jnp.dot(top_field, mid_transfer, precision=highest)
    leaf_down = jnp.dot(mid_field, leaf_transfer, precision=highest)
    leaf_field = (far_field + leaf_down).reshape(NRHS, LEAF_DEV, RANK)
    far_out = jnp.einsum("rlk,lkb->rlb", leaf_field, leaf_basis, precision=highest)
    return far_out.reshape(NRHS, LEAF_DEV * LEAF) + near_out


def solution(mesh):
    in_specs = (
        P(None, "clus"),
        P(None, "clus"),
        P("clus"),
        P("clus", None, None),
        P(None, "clus"),
        P(None, "clus"),
        P(None, "clus"),
        P(None, "clus"),
        P(),
        P("clus", None),
        P("clus"),
        P("clus", None),
        P("clus", None),
        P(),
    )
    out_specs = P(None, "clus")
    return jax.shard_map(shards, mesh=mesh, in_specs=in_specs, out_specs=out_specs, check_vma=False)
```

```python
import math

import jax
import jax.numpy as jnp
from jax import lax
from jax.experimental import pallas as pl
from jax.experimental.pallas import tpu as pltpu
from jax.sharding import PartitionSpec as P

LEAF = 256
RANK = 64
NRHS = 32
LEAF_DEV = 32
NEAR_MAX = 27
FAR2 = 16
GROUP = 8
FEAT = 48


smoothing = 0.05
inv_four_pi = 1.0 / (4.0 * math.pi)
highest = lax.Precision.HIGHEST
f32 = jnp.float32
bf16 = jnp.bfloat16


def green(source, target):
    first = source[0][..., :, None] - target[0][..., None, :]
    second = source[1][..., :, None] - target[1][..., None, :]
    third = source[2][..., :, None] - target[2][..., None, :]
    total = first * first + second * second + third * third
    return inv_four_pi / jnp.sqrt(total + smoothing * smoothing)


def rounded(value):
    return value.astype(bf16).astype(f32)


def split3(value):
    high = rounded(value)
    rest = value - high
    mid = rounded(rest)
    return high, mid, rounded(rest - mid)


def centred_rows(x, y, z, centre):
    x = x - centre[0]
    y = y - centre[1]
    z = z - centre[2]
    return x, y, z, x * x + y * y + z * z


def rows8(values):
    width = values[0].shape[1]
    row = lax.broadcasted_iota(jnp.int32, (8, width), 0)
    out = jnp.zeros((8, width), f32)
    for place, value in enumerate(values):
        out = jnp.where(row == place, value, out)
    return out


def source_features(x, y, z, centre):
    x, y, z, norm = centred_rows(x, y, z, centre)
    high, mid, low = split3(rows8([x, y, z, norm, jnp.ones_like(x)]))
    return jnp.concatenate([high, mid, low, high, mid, high], axis=0)


def target_features(x, y, z, centre):
    x, y, z, norm = centred_rows(x, y, z, centre)
    high, mid, low = split3(
        rows8([-2.0 * x, -2.0 * y, -2.0 * z, jnp.ones_like(x), norm + smoothing * smoothing])
    )
    return jnp.concatenate([high, high, high, mid, mid, low], axis=0)


def halves(value):
    high = value.astype(bf16)
    return high, (value - high.astype(f32)).astype(bf16)


def kernel_halves(features, target):
    return halves(lax.rsqrt(jnp.dot(features, target, preferred_element_type=f32)))


def apply(coef, high, low):
    first = jnp.dot(coef, high, preferred_element_type=f32)
    second = jnp.dot(coef[:NRHS], low, preferred_element_type=f32)
    return first[:NRHS] + first[NRHS:] + second


def couple(with_far, *refs):
    refs = list(refs)
    near_ref, count_ref = refs[:2]
    if with_far:
        far_ref, partial_ref, before_ref, own_ref, after_ref, near_out, far_out = refs[2:9]
        del refs[:9]
        node_source, node_target, coef_left, coef_right = refs[:4]
        del refs[:4]
        parts = [before_ref, after_ref]
    else:
        own_ref, near_out = refs[2:4]
        del refs[:4]
        parts = [own_ref]
    point_source, point_target, charge_store, high_even, low_even, high_odd, low_odd = refs
    points = LEAF_DEV * LEAF
    empty = len(parts) * LEAF_DEV
    sums = [jnp.sum(own_ref[NRHS + d : NRHS + d + 1, :points], axis=1, keepdims=True) for d in range(3)]
    centre = [total * (1.0 / points) for total in sums]
    lane = lax.broadcasted_iota(jnp.int32, (2 * NRHS, 128), 1)
    charge_store[empty] = jnp.zeros((2 * NRHS, LEAF), bf16)
    high_odd[...] = jnp.zeros_like(high_odd)
    low_odd[...] = jnp.zeros_like(low_odd)
    pairs = LEAF_DEV // 2

    for part, pack in enumerate(parts):

        def prepare(group, carry, pack=pack, part=part):
            for offset in range(4):
                leaf = group * 4 + offset
                columns = pl.ds(pl.multiple_of(leaf * LEAF, LEAF), LEAF)
                place = part * LEAF_DEV + leaf
                x, y, z, weight = [pack[NRHS + d : NRHS + d + 1, columns] for d in range(4)]
                point_source[place] = source_features(x, y, z, centre).T.astype(bf16)
                if part == 0:
                    own = [own_ref[NRHS + d : NRHS + d + 1, columns] for d in range(3)]
                    point_target[leaf] = target_features(*own, centre).astype(bf16)
                high, low = halves(pack[:NRHS, columns] * (weight * inv_four_pi))
                charge_store[place, :NRHS, :] = high
                charge_store[place, NRHS:, :] = low
            return carry

        lax.fori_loop(0, LEAF_DEV // 4, prepare, 0)

    for part, coefs in enumerate([before_ref, own_ref, after_ref] if with_far else []):

        def prepare_nodes(pair, carry, coefs=coefs, part=part):
            columns = pl.ds(pl.multiple_of(points + pair * 128, 128), 128)
            place = part * LEAF_DEV + pair * 2
            x, y, z = [coefs[NRHS + d : NRHS + d + 1, columns] for d in range(3)]
            features = source_features(x, y, z, centre).T.astype(bf16)
            node_source[place] = features[:RANK]
            node_source[place + 1] = features[RANK:]
            if part == 1:
                node_target[pair] = target_features(x, y, z, centre).astype(bf16)
            high = rounded(coefs[:NRHS, columns] * inv_four_pi)
            low = coefs[:NRHS, columns] * inv_four_pi - high
            both = jnp.concatenate([high, low], axis=0)
            turned = pltpu.roll(both, RANK, 1)
            left = lane < RANK
            coef_left[place] = jnp.where(left, both, 0.0).astype(bf16)
            coef_right[place] = jnp.where(left, 0.0, turned).astype(bf16)
            coef_left[place + 1] = jnp.where(left, turned, 0.0).astype(bf16)
            coef_right[place + 1] = jnp.where(left, 0.0, both).astype(bf16)
            return carry

        lax.fori_loop(0, pairs, prepare_nodes, 0)

    def near(leaf):
        count = count_ref[leaf]
        target = point_target[leaf]

        def stage(slot, high_ref, low_ref):
            source = near_ref[leaf, jnp.minimum(slot, NEAR_MAX - 1)]
            high_ref[...], low_ref[...] = kernel_halves(point_source[source], target)
            return jnp.where(slot < count, source, empty)

        def slots(step, carry):
            total, waiting = carry
            total = total + apply(charge_store[waiting], high_odd[...], low_odd[...])
            even = stage(step * 2, high_even, low_even)
            total = total + apply(charge_store[even], high_even[...], low_even[...])
            return total, stage(step * 2 + 1, high_odd, low_odd)

        columns = pl.ds(pl.multiple_of(leaf * LEAF, LEAF), LEAF)
        first = partial_ref[:, columns] if with_far else jnp.zeros((NRHS, LEAF), f32)
        start = (first, jnp.int32(empty))
        total, waiting = lax.fori_loop(0, (count + 1) // 2, slots, start)
        return total + apply(charge_store[waiting], high_odd[...], low_odd[...])

    def far(leaf, pair):
        sources = [far_ref[leaf, slot] for slot in range(FAR2)]
        features = jnp.concatenate([node_source[source] for source in sources], axis=0)
        coef = jnp.concatenate(
            [coef_left[sources[i]] + coef_right[sources[i + 1]] for i in range(0, FAR2, 2)], axis=1
        )
        return apply(coef, *kernel_halves(features, node_target[pair]))

    def work(pair, carry):
        for offset in range(2):
            leaf = pair * 2 + offset
            near_out[:, pl.ds(pl.multiple_of(leaf * LEAF, LEAF), LEAF)] = near(leaf)
        if not with_far:
            return carry
        even, odd = far(pair * 2, pair), far(pair * 2 + 1, pair)
        columns = pl.ds(pl.multiple_of(pair * 128, 128), 128)
        far_out[:, columns] = jnp.where(lane[:NRHS] < RANK, even, odd)
        return carry

    lax.fori_loop(0, pairs, work, 0)


def coupled(with_far, lists, arrays):
    window = (2 if with_far else 1) * LEAF_DEV
    smem = pl.BlockSpec(memory_space=pltpu.SMEM)
    vmem = pl.BlockSpec(memory_space=pltpu.VMEM)
    out_shape = [jax.ShapeDtypeStruct((NRHS, LEAF_DEV * LEAF), f32)]
    scratch = [
        pltpu.VMEM((window, LEAF, FEAT), bf16),
        pltpu.VMEM((LEAF_DEV, FEAT, LEAF), bf16),
        pltpu.VMEM((window + 1, 2 * NRHS, LEAF), bf16),
    ] + [pltpu.VMEM((LEAF, LEAF), bf16)] * 4
    if with_far:
        out_shape.append(jax.ShapeDtypeStruct((NRHS, LEAF_DEV * RANK), f32))
        scratch = [
            pltpu.VMEM((3 * LEAF_DEV, RANK, FEAT), bf16),
            pltpu.VMEM((LEAF_DEV // 2, FEAT, 128), bf16),
            pltpu.VMEM((3 * LEAF_DEV, 2 * NRHS, 128), bf16),
            pltpu.VMEM((3 * LEAF_DEV, 2 * NRHS, 128), bf16),
        ] + scratch
    return pl.pallas_call(
        lambda *refs: couple(with_far, *refs),
        out_shape=out_shape,
        in_specs=[smem] * len(lists) + [vmem] * len(arrays),
        out_specs=[vmem] * len(out_shape),
        scratch_shapes=scratch,
        compiler_params=pltpu.CompilerParams(vmem_limit_bytes=48 * 1024 * 1024),
        cost_estimate=pl.CostEstimate(
            flops=40_000_000_000, bytes_accessed=8_000_000, transcendentals=25_000_000
        ),
    )(*lists, *arrays)


def compacted(flags, values):
    slots = jnp.arange(NEAR_MAX)
    earlier = slots[None, :] < slots[:, None]
    rank = jnp.sum(flags[..., None, :] & earlier, axis=-1)
    chosen = flags[..., None, :] & (rank[..., None, :] == slots[:, None])
    lists = jnp.sum(jnp.where(chosen, values[..., None, :], 0), axis=-1)
    return lists.astype(jnp.int32), jnp.sum(flags, axis=-1).astype(jnp.int32)


def doubling(steps, block_ref, all_ref, send_sems, recv_sems):
    me = lax.axis_index("clus")
    partners = [me + (1 - 2 * ((me // 2**k) % 2)) * 2**k for k in range(steps)]
    barrier = pltpu.get_barrier_semaphore()
    for partner in partners:
        pl.semaphore_signal(
            barrier, inc=1, device_id=(partner,), device_id_type=pl.DeviceIdType.MESH
        )
    pl.semaphore_wait(barrier, steps)
    all_ref[me] = block_ref[...]
    for k, partner in enumerate(partners):
        held = all_ref.at[pl.ds((me // 2**k) * 2**k, 2**k)]
        copy = pltpu.make_async_remote_copy(
            src_ref=held,
            dst_ref=held,
            send_sem=send_sems.at[k],
            recv_sem=recv_sems.at[k],
            device_id=(partner,),
            device_id_type=pl.DeviceIdType.MESH,
        )
        copy.start()
        copy.wait()


def gathered(block):
    devices = lax.axis_size("clus")
    steps = devices.bit_length() - 1
    vmem = pl.BlockSpec(memory_space=pltpu.VMEM)
    return pl.pallas_call(
        lambda *refs: doubling(steps, *refs),
        out_shape=jax.ShapeDtypeStruct((devices,) + block.shape, f32),
        in_specs=[vmem],
        out_specs=vmem,
        scratch_shapes=[pltpu.SemaphoreType.DMA((steps,)), pltpu.SemaphoreType.DMA((steps,))],
        compiler_params=pltpu.CompilerParams(
            collective_id=0, has_side_effects=True, vmem_limit_bytes=16 * 1024 * 1024
        ),
        cost_estimate=pl.CostEstimate(flops=0, bytes_accessed=20_000_000, transcendentals=0),
    )(block)


def around(array):
    size = lax.axis_size("clus")
    up = [(i, (i + 1) % size) for i in range(size)]
    down = [(j, i) for i, j in up]
    return lax.ppermute(array, "clus", up), array, lax.ppermute(array, "clus", down)


def shards(
    charges,
    positions,
    quad_weights,
    leaf_basis,
    leaf_nodes,
    leaf_transfer,
    mid_nodes,
    mid_transfer,
    top_nodes,
    near_list,
    near_count,
    far_list,
    mid_mask,
    top_mask,
):
    devices = lax.axis_size("clus")
    myself = lax.axis_index("clus")
    all_leaves = LEAF_DEV * devices
    top_count = devices // GROUP
    point_pack = jnp.concatenate([charges, positions, quad_weights[None, :]], axis=0)
    leaf_charges = charges.reshape(NRHS, LEAF_DEV, LEAF)
    leaf_coef = jnp.einsum("rlb,lkb->rlk", leaf_charges, leaf_basis, precision=highest)
    coef_flat = leaf_coef.reshape(NRHS, LEAF_DEV * RANK)
    coef_pack = jnp.concatenate([coef_flat, leaf_nodes, jnp.zeros_like(leaf_nodes[:1])], axis=0)
    packs = around(jnp.concatenate([point_pack, coef_pack], axis=1))

    first_leaf = myself * LEAF_DEV - LEAF_DEV
    near_local = (near_list - first_leaf) % all_leaves
    far_local = (far_list - first_leaf) % all_leaves
    live = jnp.arange(NEAR_MAX) < near_count[:, None]
    own = (near_local >= LEAF_DEV) & (near_local < 2 * LEAF_DEV)
    place = jnp.where(near_local < LEAF_DEV, near_local, near_local - LEAF_DEV)
    lists, counts = compacted(jnp.stack([live & own, live & ~own]), jnp.stack([place, place]))
    (partial,) = coupled(False, (lists[0], counts[0]), (packs[1],))
    contract_last = (((1,), (1,)), ((), ()))
    mid_coef = lax.dot_general(coef_flat, leaf_transfer, contract_last, precision=highest)
    upward = lax.dot_general(mid_coef, mid_transfer, contract_last, precision=highest)
    level_pack = jnp.concatenate([mid_coef, upward], axis=1)
    level_pack = jnp.concatenate([level_pack, jnp.pad(mid_nodes, ((0, 5), (0, RANK)))], axis=0)
    level_pack, partial = lax.optimization_barrier((level_pack, partial))
    everyone = gathered(level_pack)
    near_out, far_field = coupled(True, (lists[1], counts[1], far_local), (partial,) + packs)

    all_coef = everyone[:, :NRHS, :RANK].transpose(1, 0, 2).reshape(NRHS, devices * RANK)
    all_upward = everyone[:, :NRHS, RANK:].reshape(top_count, GROUP, NRHS, RANK)
    all_nodes = everyone[:, NRHS : NRHS + 3, :RANK].transpose(1, 0, 2).reshape(3, devices * RANK)
    top_coef = all_upward.sum(axis=1).transpose(1, 0, 2).reshape(NRHS, top_count * RANK)
    parent = myself // GROUP
    top_target = lax.dynamic_slice_in_dim(top_nodes, parent * RANK, RANK, 1)
    top_row = lax.dynamic_index_in_dim(top_mask, parent, 0, keepdims=False)
    top_select = jnp.repeat(top_row.astype(jnp.float32), RANK)[:, None]
    top_field = jnp.dot(top_coef, green(top_nodes, top_target) * top_select, precision=highest)
    mid_select = jnp.repeat(mid_mask[0].astype(jnp.float32), RANK)[:, None]
    mid_field = jnp.dot(all_coef, green(all_nodes, mid_nodes) * mid_select, precision=highest)
    mid_field = mid_field + jnp.dot(top_field, mid_transfer, precision=highest)
    leaf_down = jnp.dot(mid_field, leaf_transfer, precision=highest)
    leaf_field = (far_field + leaf_down).reshape(NRHS, LEAF_DEV, RANK)
    far_out = jnp.einsum("rlk,lkb->rlb", leaf_field, leaf_basis, precision=highest)
    return far_out.reshape(NRHS, LEAF_DEV * LEAF) + near_out


def solution(mesh):
    in_specs = (
        P(None, "clus"),
        P(None, "clus"),
        P("clus"),
        P("clus", None, None),
        P(None, "clus"),
        P(None, "clus"),
        P(None, "clus"),
        P(None, "clus"),
        P(),
        P("clus", None),
        P("clus"),
        P("clus", None),
        P("clus", None),
        P(),
    )
    out_specs = P(None, "clus")
    return jax.shard_map(shards, mesh=mesh, in_specs=in_specs, out_specs=out_specs, check_vma=False)
```

```python
import math

import jax
import jax.numpy as jnp
from jax import lax
from jax.experimental import pallas as pl
from jax.experimental.pallas import tpu as pltpu
from jax.sharding import PartitionSpec as P

LEAF = 256
RANK = 64
NRHS = 32
LEAF_DEV = 32
NEAR_MAX = 27
FAR2 = 16
GROUP = 8
FEAT = 48


smoothing = 0.05
inv_four_pi = 1.0 / (4.0 * math.pi)
highest = lax.Precision.HIGHEST
f32 = jnp.float32
bf16 = jnp.bfloat16


def green(source, target):
    first = source[0][..., :, None] - target[0][..., None, :]
    second = source[1][..., :, None] - target[1][..., None, :]
    third = source[2][..., :, None] - target[2][..., None, :]
    total = first * first + second * second + third * third
    return inv_four_pi / jnp.sqrt(total + smoothing * smoothing)


def rounded(value):
    return value.astype(bf16).astype(f32)


def split3(value):
    high = rounded(value)
    rest = value - high
    mid = rounded(rest)
    return high, mid, rounded(rest - mid)


def centred_rows(x, y, z, centre):
    x = x - centre[0]
    y = y - centre[1]
    z = z - centre[2]
    return x, y, z, x * x + y * y + z * z


def rows8(values):
    width = values[0].shape[1]
    row = lax.broadcasted_iota(jnp.int32, (8, width), 0)
    out = jnp.zeros((8, width), f32)
    for place, value in enumerate(values):
        out = jnp.where(row == place, value, out)
    return out


def source_features(x, y, z, centre):
    x, y, z, norm = centred_rows(x, y, z, centre)
    high, mid, low = split3(rows8([x, y, z, norm, jnp.ones_like(x)]))
    return jnp.concatenate([high, mid, low, high, mid, high], axis=0)


def target_features(x, y, z, centre):
    x, y, z, norm = centred_rows(x, y, z, centre)
    high, mid, low = split3(
        rows8([-2.0 * x, -2.0 * y, -2.0 * z, jnp.ones_like(x), norm + smoothing * smoothing])
    )
    return jnp.concatenate([high, high, high, mid, mid, low], axis=0)


def halves(value):
    high = value.astype(bf16)
    return high, (value - high.astype(f32)).astype(bf16)


def kernel_halves(features, target):
    return halves(lax.rsqrt(jnp.dot(features, target, preferred_element_type=f32)))


def apply(coef, high, low):
    first = jnp.dot(coef, high, preferred_element_type=f32)
    second = jnp.dot(coef[:NRHS], low, preferred_element_type=f32)
    return first[:NRHS] + first[NRHS:] + second


def couple(with_far, *refs):
    refs = list(refs)
    near_ref, count_ref = refs[:2]
    if with_far:
        far_ref, partial_ref, before_ref, own_ref, after_ref, near_out, far_out = refs[2:9]
        del refs[:9]
        node_source, node_target, coef_left, coef_right = refs[:4]
        del refs[:4]
        parts = [before_ref, after_ref]
    else:
        own_ref, near_out = refs[2:4]
        del refs[:4]
        parts = [own_ref]
    point_source, point_target, charge_store, high_even, low_even, high_odd, low_odd = refs
    points = LEAF_DEV * LEAF
    empty = len(parts) * LEAF_DEV
    sums = [jnp.sum(own_ref[NRHS + d : NRHS + d + 1, :points], axis=1, keepdims=True) for d in range(3)]
    centre = [total * (1.0 / points) for total in sums]
    lane = lax.broadcasted_iota(jnp.int32, (2 * NRHS, 128), 1)
    charge_store[empty] = jnp.zeros((2 * NRHS, LEAF), bf16)
    high_odd[...] = jnp.zeros_like(high_odd)
    low_odd[...] = jnp.zeros_like(low_odd)
    pairs = LEAF_DEV // 2

    for part, pack in enumerate(parts):

        def prepare(group, carry, pack=pack, part=part):
            for offset in range(4):
                leaf = group * 4 + offset
                columns = pl.ds(pl.multiple_of(leaf * LEAF, LEAF), LEAF)
                place = part * LEAF_DEV + leaf
                x, y, z, weight = [pack[NRHS + d : NRHS + d + 1, columns] for d in range(4)]
                point_source[place] = source_features(x, y, z, centre).T.astype(bf16)
                if part == 0:
                    own = [own_ref[NRHS + d : NRHS + d + 1, columns] for d in range(3)]
                    point_target[leaf] = target_features(*own, centre).astype(bf16)
                high, low = halves(pack[:NRHS, columns] * (weight * inv_four_pi))
                charge_store[place, :NRHS, :] = high
                charge_store[place, NRHS:, :] = low
            return carry

        lax.fori_loop(0, LEAF_DEV // 4, prepare, 0)

    for part, coefs in enumerate([before_ref, own_ref, after_ref] if with_far else []):

        def prepare_nodes(pair, carry, coefs=coefs, part=part):
            columns = pl.ds(pl.multiple_of(points + pair * 128, 128), 128)
            place = part * LEAF_DEV + pair * 2
            x, y, z = [coefs[NRHS + d : NRHS + d + 1, columns] for d in range(3)]
            features = source_features(x, y, z, centre).T.astype(bf16)
            node_source[place] = features[:RANK]
            node_source[place + 1] = features[RANK:]
            if part == 1:
                node_target[pair] = target_features(x, y, z, centre).astype(bf16)
            high = rounded(coefs[:NRHS, columns] * inv_four_pi)
            low = coefs[:NRHS, columns] * inv_four_pi - high
            both = jnp.concatenate([high, low], axis=0)
            turned = pltpu.roll(both, RANK, 1)
            left = lane < RANK
            coef_left[place] = jnp.where(left, both, 0.0).astype(bf16)
            coef_right[place] = jnp.where(left, 0.0, turned).astype(bf16)
            coef_left[place + 1] = jnp.where(left, turned, 0.0).astype(bf16)
            coef_right[place + 1] = jnp.where(left, 0.0, both).astype(bf16)
            return carry

        lax.fori_loop(0, pairs, prepare_nodes, 0)

    def near(leaf):
        count = count_ref[leaf]
        target = point_target[leaf]

        def stage(slot, high_ref, low_ref):
            source = near_ref[leaf, jnp.minimum(slot, NEAR_MAX - 1)]
            high_ref[...], low_ref[...] = kernel_halves(point_source[source], target)
            return jnp.where(slot < count, source, empty)

        def slots(step, carry):
            total, waiting = carry
            total = total + apply(charge_store[waiting], high_odd[...], low_odd[...])
            even = stage(step * 2, high_even, low_even)
            total = total + apply(charge_store[even], high_even[...], low_even[...])
            return total, stage(step * 2 + 1, high_odd, low_odd)

        columns = pl.ds(pl.multiple_of(leaf * LEAF, LEAF), LEAF)
        first = partial_ref[:, columns] if with_far else jnp.zeros((NRHS, LEAF), f32)
        start = (first, jnp.int32(empty))
        total, waiting = lax.fori_loop(0, (count + 1) // 2, slots, start)
        return total + apply(charge_store[waiting], high_odd[...], low_odd[...])

    def far(leaf, pair):
        sources = [far_ref[leaf, slot] for slot in range(FAR2)]
        features = jnp.concatenate([node_source[source] for source in sources], axis=0)
        coef = jnp.concatenate(
            [coef_left[sources[i]] + coef_right[sources[i + 1]] for i in range(0, FAR2, 2)], axis=1
        )
        return apply(coef, *kernel_halves(features, node_target[pair]))

    def work(pair, carry):
        for offset in range(2):
            leaf = pair * 2 + offset
            near_out[:, pl.ds(pl.multiple_of(leaf * LEAF, LEAF), LEAF)] = near(leaf)
        if not with_far:
            return carry
        even, odd = far(pair * 2, pair), far(pair * 2 + 1, pair)
        columns = pl.ds(pl.multiple_of(pair * 128, 128), 128)
        far_out[:, columns] = jnp.where(lane[:NRHS] < RANK, even, odd)
        return carry

    lax.fori_loop(0, pairs, work, 0)


def coupled(with_far, lists, arrays):
    window = (2 if with_far else 1) * LEAF_DEV
    smem = pl.BlockSpec(memory_space=pltpu.SMEM)
    vmem = pl.BlockSpec(memory_space=pltpu.VMEM)
    out_shape = [jax.ShapeDtypeStruct((NRHS, LEAF_DEV * LEAF), f32)]
    scratch = [
        pltpu.VMEM((window, LEAF, FEAT), bf16),
        pltpu.VMEM((LEAF_DEV, FEAT, LEAF), bf16),
        pltpu.VMEM((window + 1, 2 * NRHS, LEAF), bf16),
    ] + [pltpu.VMEM((LEAF, LEAF), bf16)] * 4
    if with_far:
        out_shape.append(jax.ShapeDtypeStruct((NRHS, LEAF_DEV * RANK), f32))
        scratch = [
            pltpu.VMEM((3 * LEAF_DEV, RANK, FEAT), bf16),
            pltpu.VMEM((LEAF_DEV // 2, FEAT, 128), bf16),
            pltpu.VMEM((3 * LEAF_DEV, 2 * NRHS, 128), bf16),
            pltpu.VMEM((3 * LEAF_DEV, 2 * NRHS, 128), bf16),
        ] + scratch
    return pl.pallas_call(
        lambda *refs: couple(with_far, *refs),
        out_shape=out_shape,
        in_specs=[smem] * len(lists) + [vmem] * len(arrays),
        out_specs=[vmem] * len(out_shape),
        scratch_shapes=scratch,
        compiler_params=pltpu.CompilerParams(vmem_limit_bytes=48 * 1024 * 1024),
        cost_estimate=pl.CostEstimate(
            flops=40_000_000_000, bytes_accessed=8_000_000, transcendentals=25_000_000
        ),
    )(*lists, *arrays)


def compacted(flags, values):
    slots = jnp.arange(NEAR_MAX)
    earlier = slots[None, :] < slots[:, None]
    rank = jnp.sum(flags[..., None, :] & earlier, axis=-1)
    chosen = flags[..., None, :] & (rank[..., None, :] == slots[:, None])
    lists = jnp.sum(jnp.where(chosen, values[..., None, :], 0), axis=-1)
    return lists.astype(jnp.int32), jnp.sum(flags, axis=-1).astype(jnp.int32)


def doubling(steps, block_ref, out_ref, all_ref, send_sems, recv_sems):
    me = lax.axis_index("clus")
    order = list(reversed(range(steps)))
    partners = [me + (1 - 2 * ((me // 2**k) % 2)) * 2**k for k in order]
    place = sum(((me // 2**k) % 2) * 2 ** (steps - 1 - k) for k in order)
    barrier = pltpu.get_barrier_semaphore()
    for partner in partners:
        pl.semaphore_signal(
            barrier, inc=1, device_id=(partner,), device_id_type=pl.DeviceIdType.MESH
        )
    pl.semaphore_wait(barrier, steps)
    all_ref[place] = block_ref[...]
    for k, partner in enumerate(partners):
        held = all_ref.at[pl.ds((place // 2**k) * 2**k, 2**k)]
        copy = pltpu.make_async_remote_copy(
            src_ref=held,
            dst_ref=held,
            send_sem=send_sems.at[k],
            recv_sem=recv_sems.at[k],
            device_id=(partner,),
            device_id_type=pl.DeviceIdType.MESH,
        )
        copy.start()
        copy.wait()
    for device in range(2**steps):
        out_ref[device] = all_ref[sum(((device >> k) & 1) << (steps - 1 - k) for k in order)]


def gathered(block):
    devices = lax.axis_size("clus")
    steps = devices.bit_length() - 1
    vmem = pl.BlockSpec(memory_space=pltpu.VMEM)
    return pl.pallas_call(
        lambda *refs: doubling(steps, *refs),
        out_shape=jax.ShapeDtypeStruct((devices,) + block.shape, f32),
        in_specs=[vmem],
        out_specs=vmem,
        scratch_shapes=[
            pltpu.VMEM((devices,) + block.shape, f32),
            pltpu.SemaphoreType.DMA((steps,)),
            pltpu.SemaphoreType.DMA((steps,)),
        ],
        compiler_params=pltpu.CompilerParams(
            collective_id=0, has_side_effects=True, vmem_limit_bytes=16 * 1024 * 1024
        ),
        cost_estimate=pl.CostEstimate(flops=0, bytes_accessed=20_000_000, transcendentals=0),
    )(block)


def around(array):
    size = lax.axis_size("clus")
    up = [(i, (i + 1) % size) for i in range(size)]
    down = [(j, i) for i, j in up]
    return lax.ppermute(array, "clus", up), array, lax.ppermute(array, "clus", down)


def shards(
    charges,
    positions,
    quad_weights,
    leaf_basis,
    leaf_nodes,
    leaf_transfer,
    mid_nodes,
    mid_transfer,
    top_nodes,
    near_list,
    near_count,
    far_list,
    mid_mask,
    top_mask,
):
    devices = lax.axis_size("clus")
    myself = lax.axis_index("clus")
    all_leaves = LEAF_DEV * devices
    top_count = devices // GROUP
    point_pack = jnp.concatenate([charges, positions, quad_weights[None, :]], axis=0)
    leaf_charges = charges.reshape(NRHS, LEAF_DEV, LEAF)
    leaf_coef = jnp.einsum("rlb,lkb->rlk", leaf_charges, leaf_basis, precision=highest)
    coef_flat = leaf_coef.reshape(NRHS, LEAF_DEV * RANK)
    coef_pack = jnp.concatenate([coef_flat, leaf_nodes, jnp.zeros_like(leaf_nodes[:1])], axis=0)
    packs = around(jnp.concatenate([point_pack, coef_pack], axis=1))

    first_leaf = myself * LEAF_DEV - LEAF_DEV
    near_local = (near_list - first_leaf) % all_leaves
    far_local = (far_list - first_leaf) % all_leaves
    live = jnp.arange(NEAR_MAX) < near_count[:, None]
    own = (near_local >= LEAF_DEV) & (near_local < 2 * LEAF_DEV)
    place = jnp.where(near_local < LEAF_DEV, near_local, near_local - LEAF_DEV)
    lists, counts = compacted(jnp.stack([live & own, live & ~own]), jnp.stack([place, place]))
    (partial,) = coupled(False, (lists[0], counts[0]), (packs[1],))
    contract_last = (((1,), (1,)), ((), ()))
    mid_coef = lax.dot_general(coef_flat, leaf_transfer, contract_last, precision=highest)
    upward = lax.dot_general(mid_coef, mid_transfer, contract_last, precision=highest)
    level_pack = jnp.concatenate([mid_coef, upward], axis=1)
    level_pack = jnp.concatenate([level_pack, jnp.pad(mid_nodes, ((0, 5), (0, RANK)))], axis=0)
    level_pack, partial = lax.optimization_barrier((level_pack, partial))
    everyone = gathered(level_pack)
    near_out, far_field = coupled(True, (lists[1], counts[1], far_local), (partial,) + packs)

    all_coef = everyone[:, :NRHS, :RANK].transpose(1, 0, 2).reshape(NRHS, devices * RANK)
    all_upward = everyone[:, :NRHS, RANK:].reshape(top_count, GROUP, NRHS, RANK)
    all_nodes = everyone[:, NRHS : NRHS + 3, :RANK].transpose(1, 0, 2).reshape(3, devices * RANK)
    top_coef = all_upward.sum(axis=1).transpose(1, 0, 2).reshape(NRHS, top_count * RANK)
    parent = myself // GROUP
    top_target = lax.dynamic_slice_in_dim(top_nodes, parent * RANK, RANK, 1)
    top_row = lax.dynamic_index_in_dim(top_mask, parent, 0, keepdims=False)
    top_select = jnp.repeat(top_row.astype(jnp.float32), RANK)[:, None]
    top_field = jnp.dot(top_coef, green(top_nodes, top_target) * top_select, precision=highest)
    mid_select = jnp.repeat(mid_mask[0].astype(jnp.float32), RANK)[:, None]
    mid_field = jnp.dot(all_coef, green(all_nodes, mid_nodes) * mid_select, precision=highest)
    mid_field = mid_field + jnp.dot(top_field, mid_transfer, precision=highest)
    leaf_down = jnp.dot(mid_field, leaf_transfer, precision=highest)
    leaf_field = (far_field + leaf_down).reshape(NRHS, LEAF_DEV, RANK)
    far_out = jnp.einsum("rlk,lkb->rlb", leaf_field, leaf_basis, precision=highest)
    return far_out.reshape(NRHS, LEAF_DEV * LEAF) + near_out


def solution(mesh):
    in_specs = (
        P(None, "clus"),
        P(None, "clus"),
        P("clus"),
        P("clus", None, None),
        P(None, "clus"),
        P(None, "clus"),
        P(None, "clus"),
        P(None, "clus"),
        P(),
        P("clus", None),
        P("clus"),
        P("clus", None),
        P("clus", None),
        P(),
    )
    out_specs = P(None, "clus")
    return jax.shard_map(shards, mesh=mesh, in_specs=in_specs, out_specs=out_specs, check_vma=False)
```
